32 devices in a mesh: grp: 4 (over y, core), dev: 8 (over z, x).
Axes of the slice: x: 2, y: 2, z: 4, core: 2. Of those that a mesh axis runs over, the one named last changes fastest.
Arguments:
- blocks: bfloat16 [4, 8, 12, 64, 1728], P('grp', 'dev'), may hold values from -0.75 to 0.75
- prolong: bfloat16 [4, 8, 12, 64, 256], P('grp', 'dev'), may hold values from -0.75 to 0.75
- block_cols: int32 [4, 8, 12, 27], P('grp', 'dev'), may hold values from -1 to 23, as said below
- fetch_rows: int32 [4, 8, 8, 3], P('grp', 'dev'), may hold values from 0 to 11
- tile_slot: int32 [4, 8, 12, 27], P('grp', 'dev'), may hold values from 0 to 3
- tile_owner: int32 [4, 8, 4], P('grp', 'dev'), may hold values from 0 to 31, as said below
- tile_place: int32 [4, 8, 4], P('grp', 'dev'), may hold values from 0 to 1
Outputs:
- coarse: float32 [4, 8, 2, 256, 256], P('grp', 'dev')
The draws below stay inside these ranges and needn't reach their ends.
Inputs may be any that keep to these rules, and one draw needn't show every extreme that they name: `block_cols`: -1 marks a padded block slot; at most 243 slots of one device are not padding, exactly 243 on the first device. `tile_owner`: the 4 tiles of one device go to owners of distinct dev indices; at most 1 of them go to owners in one group, exactly 1 to the device's own group.
All inputs are finite; a program needn't handle non-finite values.
Results may differ from the reference program's by a relative error of at most 0.004.
Values may be sent and summed in bfloat16 or wider, within the bound.
A program may use at most 128 MiB of HBM per device.

```python
import jax
import jax.numpy as jnp
from jax import lax

BLOCK = 64
W = 256
R = 12
K = 27
CT = 2
NCAP = 3
LIVE = 243
LT = 4
N_GRP = 4
N_DEV = 8


def draw_block_cols(key, part):

    def one_device(device_key, first_flag):
        key_count, key_rank, key_cols = jax.random.split(device_key, 3)
        live_count = LIVE - jax.random.randint(key_count, (), 0, LIVE // 2 + 1)
        live_count = jnp.where(first_flag, LIVE, live_count)
        ranking = jax.random.permutation(key_rank, R * K)
        column_ids = jax.random.randint(key_cols, (R * K,), 0, N_DEV * NCAP)
        return jnp.where(ranking < live_count, column_ids, -1).reshape(R, K)
    device_keys = jax.random.split(jax.random.fold_in(key, 11), N_GRP * N_DEV)
    first_flags = jnp.arange(N_GRP * N_DEV) == 0
    result = jax.vmap(one_device)(device_keys, first_flags)
    return result.reshape(N_GRP, N_DEV, R, K).astype(jnp.int32)


def draw_tile_owner(key, part):

    def one_device(device_key, group_id):
        key_devs, key_offsets = jax.random.split(device_key, 2)
        dev_ids = jax.random.permutation(key_devs, N_DEV)[:LT]
        position = jnp.arange(LT)
        offsets = jnp.where(position < LT // 4, 0, 1 + (position - LT // 4) % (N_GRP - 1))
        offsets = jax.random.permutation(key_offsets, offsets)
        return (group_id + offsets) % N_GRP * N_DEV + dev_ids
    device_keys = jax.random.split(jax.random.fold_in(key, 23), N_GRP * N_DEV)
    group_ids = jnp.repeat(jnp.arange(N_GRP), N_DEV)
    result = jax.vmap(one_device)(device_keys, group_ids)
    return result.reshape(N_GRP, N_DEV, LT).astype(jnp.int32)


def plant(values, key, smallest, high):
    extent = values.shape
    index_at = [jax.random.randint(jax.random.fold_in(key, axis), (), 0, extent[axis]) for axis in range(len(extent))]
    values = values.at[tuple(index_at)].set(smallest)
    longest = extent.index(max(extent))
    index_at[longest] = (index_at[longest] + 1) % extent[longest]
    return values.at[tuple(index_at)].set(high)


def block_levels(stream_key, extent, pieces, smallest, high):
    def one(axis_at, shards_of):
        steps = jax.random.uniform(jax.random.fold_in(jax.random.fold_in(stream_key, 6), axis_at), (shards_of,), jnp.float32, smallest / len(pieces), high / len(pieces))
        return jnp.repeat(jnp.exp(steps), extent[axis_at] // shards_of).reshape((-1,) + (1,) * (len(extent) - axis_at - 1))

    level = one(*pieces[0])
    for cut in pieces[1:]:
        level = level * one(*cut)
    return level


def noise(rng, extent, scale, reach, cuts=(), kind=jnp.bfloat16):
    values = scale * jax.random.normal(rng, extent, jnp.float32)
    if cuts:
        values = values * block_levels(rng, extent, cuts, -0.22, 0.18)
    return jnp.clip(values, -reach, reach).astype(kind)


def setup_inputs(seed: int = 0) -> dict:
    streams_of = jax.random.split(jax.random.key(seed), 8)
    return {
        "blocks": noise(streams_of[0], (N_GRP, N_DEV, R, BLOCK, K * BLOCK), BLOCK ** -0.5, 0.75, ((0, 4), (1, 8))),
        "prolong": noise(streams_of[1], (N_GRP, N_DEV, R, BLOCK, W), BLOCK ** -0.5, 0.75, ((0, 4), (1, 8))),
        "block_cols": draw_block_cols(jax.random.fold_in(streams_of[7], 71), 0),
        "fetch_rows": plant(jax.random.randint(streams_of[3], (N_GRP, N_DEV, N_DEV, NCAP), 0, R), jax.random.fold_in(streams_of[3], 1), 0, R - 1).astype(jnp.int32),
        "tile_slot": plant(jax.random.randint(streams_of[4], (N_GRP, N_DEV, R, K), 0, LT), jax.random.fold_in(streams_of[4], 1), 0, LT - 1).astype(jnp.int32),
        "tile_owner": draw_tile_owner(jax.random.fold_in(streams_of[7], 71), 0),
        "tile_place": plant(jax.random.randint(streams_of[6], (N_GRP, N_DEV, LT), 0, CT), jax.random.fold_in(streams_of[6], 1), 0, CT - 1).astype(jnp.int32),
    }


def device_tiles(row_blocks, row_panels, row_columns, row_slots, arrived):
    def one_row(running, item):
        block_row, panel_row, column_ids, slot_ids = item
        matrix = block_row.reshape(BLOCK, K, BLOCK).astype(jnp.float32)
        near_panels = arrived[jnp.maximum(column_ids, 0)].astype(jnp.float32)
        product = jnp.einsum("rkc,kcw->krw", matrix, near_panels)
        product = jnp.where((column_ids >= 0)[:, None, None], product, 0.0).astype(jnp.bfloat16)
        outer_tile = jnp.einsum("ra,krb->kab", panel_row.astype(jnp.float32), product.astype(jnp.float32))
        return running.at[slot_ids].add(outer_tile), None

    running = jnp.zeros((LT, W, W), jnp.float32)
    running, unused = lax.scan(one_row, running, (row_blocks, row_panels, row_columns, row_slots))
    return running.astype(jnp.bfloat16)


def reference(blocks, prolong, block_cols, fetch_rows, tile_slot, tile_owner, tile_place):
    coarse_sum = jnp.zeros((N_GRP * N_DEV * CT, W, W), jnp.float32)

    def per_device(running, flat_index):
        group_id = flat_index // N_DEV
        device_id = flat_index % N_DEV
        chosen = fetch_rows[group_id][:, device_id, :]
        group_panels = prolong[group_id]
        arrived = group_panels[jnp.arange(N_DEV, dtype=jnp.int32)[:, None], chosen]
        arrived = arrived.reshape(N_DEV * NCAP, BLOCK, W)
        partial_value = device_tiles(blocks[group_id, device_id], group_panels[device_id],
                               block_cols[group_id, device_id], tile_slot[group_id, device_id], arrived)
        target_ids = tile_owner[group_id, device_id] * CT + tile_place[group_id, device_id]
        return running.at[target_ids].add(partial_value.astype(jnp.float32)), None

    coarse_sum, unused = lax.scan(per_device, coarse_sum, jnp.arange(N_GRP * N_DEV, dtype=jnp.int32))
    return coarse_sum.reshape(N_GRP, N_DEV, CT, W, W)
```

```python
import functools

import jax
import jax.numpy as jnp
from jax import lax
from jax.experimental import pallas as pl
from jax.experimental.pallas import tpu as pltpu
from jax.sharding import PartitionSpec as P

BLOCK = 64
W = 256
K = 27
CT = 2
NCAP = 3


def pick(panels, ids):
    ones = (ids[..., None] == jnp.arange(panels.shape[0], dtype=jnp.int32)).astype(panels.dtype)
    return jnp.einsum(
        "...p,prw->...rw", ones, panels, preferred_element_type=jnp.float32
    ).astype(panels.dtype)


def plain_body(blocks, prolong, block_cols, fetch_rows, tile_slot, tile_owner, tile_place):
    dev_count = lax.axis_size("dev")
    grp_count = lax.axis_size("grp")
    panels = prolong[0, 0]
    chosen = fetch_rows[0, 0]
    outgoing = pick(panels, chosen)
    arrived = lax.all_to_all(outgoing, "dev", split_axis=0, concat_axis=0, tiled=True)
    arrived = arrived.reshape(dev_count * NCAP, BLOCK, W)
    owners = tile_owner[0, 0]
    places = tile_place[0, 0]
    local_count = owners.shape[0]
    tile_range = jnp.arange(local_count, dtype=jnp.int32)

    def one_row(running, item):
        block_row, panel_row, column_ids, slot_ids = item
        matrix = block_row.reshape(BLOCK, K, BLOCK)
        near_panels = pick(arrived, column_ids)
        product = jnp.einsum(
            "rkc,kcw->krw", matrix, near_panels, preferred_element_type=jnp.float32
        )
        product = jnp.where((column_ids >= 0)[:, None, None], product, 0.0).astype(jnp.bfloat16)
        outer_tile = jnp.einsum(
            "ra,krb->kab", panel_row, product, preferred_element_type=jnp.float32
        )
        selector = (slot_ids[:, None] == tile_range[None, :]).astype(jnp.float32)
        added = jnp.einsum("kt,kab->tab", selector, outer_tile, precision=lax.Precision.HIGHEST)
        return (running + added, None)

    running = jnp.zeros((local_count, W, W), jnp.float32)
    running, unused = lax.scan(
        one_row, running, (blocks[0, 0], panels, block_cols[0, 0], tile_slot[0, 0])
    )
    partial_value = running.astype(jnp.bfloat16)
    dev_target = owners % dev_count
    grp_target = owners // dev_count
    sending = jnp.zeros((dev_count, W, W), jnp.bfloat16).at[dev_target].set(partial_value)
    labels = jnp.full((dev_count,), -1, jnp.int32).at[dev_target].set(grp_target * CT + places)
    got_tiles, got_labels = (
        lax.all_to_all(sending, "dev", split_axis=0, concat_axis=0, tiled=True),
        lax.all_to_all(labels, "dev", split_axis=0, concat_axis=0, tiled=True),
    )
    spread = grp_count * CT
    keyed = jnp.where(got_labels >= 0, got_labels, spread)
    table = (
        jnp.zeros((spread, W, W), jnp.float32)
        .at[keyed]
        .add(got_tiles.astype(jnp.float32), mode="drop")
    )
    result = lax.psum_scatter(table, "grp", scatter_dimension=0, tiled=True)
    return result.reshape(1, 1, CT, W, W)


MESH = pl.DeviceIdType.MESH
HALVES = 2
LABEL_ROWS = 16


def kernel(
    n_grp, n_dev, prolong_ref, cols_ref, fetch_ref, slot_ref, owner_ref, place_ref, blocks_ref,
    out_ref,
    mat, fetched, stage1, spread, near, high, low, panels_t, part, stage2, got2, stage3, got3, mine,
    blocks_sem, send1, recv1, send2, recv2, send3, recv3,
):
    rows = blocks_ref.shape[0]
    slots = cols_ref.shape[1]
    tiles = owner_ref.shape[0]
    ncap = fetch_ref.shape[1]
    sub = BLOCK // LABEL_ROWS
    piece = ncap * sub + 1
    half = W // HALVES
    g = lax.axis_index("grp")
    d = lax.axis_index("dev")
    load = pltpu.make_async_copy(blocks_ref, mat, blocks_sem)
    load.start()

    barrier = pltpu.get_barrier_semaphore()
    for j in range(1, n_dev):
        pl.semaphore_signal(barrier, inc=1, device_id=(g, lax.rem(d + j, n_dev)), device_id_type=MESH)
    for j in range(1, n_grp):
        pl.semaphore_signal(barrier, inc=1, device_id=(lax.rem(g + j, n_grp), d), device_id_type=MESH)

    def tile_for(target):
        found = jnp.int32(tiles)
        label = jnp.int32(-1)
        for t in range(tiles):
            hit = lax.rem(owner_ref[t], n_dev) == target
            found = jnp.where(hit, t, found)
            label = jnp.where(hit, lax.div(owner_ref[t], n_dev) * CT + place_ref[t], label)
        return found, label

    def fill(where, target, base, label):
        for c in range(ncap):
            panel = prolong_ref[fetch_ref[target, c]]
            where[pl.ds(base + c * sub, sub)] = panel.reshape(sub, LABEL_ROWS, W)
        tag = jnp.full((1, LABEL_ROWS, W), label.astype(jnp.float32), jnp.float32)
        where[pl.ds(base + ncap * sub, 1)] = tag.astype(jnp.bfloat16)

    found = [None] * n_dev
    for j in range(n_dev):
        target = lax.rem(d + j, n_dev)
        found[j], label = tile_for(target)
        if j == 0:
            fill(fetched, target, d * piece, label)
        else:
            fill(stage1.at[j], target, 0, label)

    pl.semaphore_wait(barrier, n_dev - 1 + n_grp - 1)
    first = []
    for j in far_first(n_dev):
        copy = pltpu.make_async_remote_copy(
            src_ref=stage1.at[j],
            dst_ref=fetched.at[pl.ds(d * piece, piece)],
            send_sem=send1.at[j],
            recv_sem=recv1.at[j],
            device_id=(g, lax.rem(d + j, n_dev)),
            device_id_type=MESH,
        )
        copy.start()
        first.append(copy)

    panels_t[...] = prolong_ref[...].reshape(rows * BLOCK, W).T
    for h in range(HALVES):
        part[h, tiles] = jnp.zeros((half, W), jnp.bfloat16)
    load.wait()
    lane = lax.broadcasted_iota(jnp.int32, (1, 2 * BLOCK), 1)

    def place_blocks(i, unused):
        for k in range(0, slots, 2):
            width = min(2, slots - k) * BLOCK
            ids = [
                jnp.where(cols_ref[i, m] >= 0, slot_ref[i, m], -1)
                for m in range(k, min(k + 2, slots))
            ]
            ids = jnp.where(lane < BLOCK, ids[0], ids[-1])[:, :width]
            at = slice(k * BLOCK, k * BLOCK + width)
            values = mat[i, :, at]
            for t in range(tiles):
                mask = jnp.where(ids == t, 1.0, 0.0).astype(jnp.bfloat16)
                spread[i, t * BLOCK : (t + 1) * BLOCK, at] = values * mask
        return unused

    lax.fori_loop(0, rows, place_blocks, 0)
    for copy in first:
        copy.wait()

    def one_row(i, unused):
        for k in range(slots):
            col = jnp.maximum(cols_ref[i, k], 0)
            panel = fetched[pl.ds(col * sub + lax.div(col, ncap), sub)]
            near[k * BLOCK : (k + 1) * BLOCK, :] = panel.reshape(BLOCK, W)
        total = jnp.dot(spread[i], near[...], preferred_element_type=jnp.float32)
        top = total.astype(jnp.bfloat16)
        rest = (total - top.astype(jnp.float32)).astype(jnp.bfloat16)
        at = pl.ds(pl.multiple_of(i * BLOCK, BLOCK), BLOCK)
        for t in range(tiles):
            high[t, at, :] = top[t * BLOCK : (t + 1) * BLOCK]
            low[t, at, :] = rest[t * BLOCK : (t + 1) * BLOCK]
        return unused

    lax.fori_loop(0, rows, one_row, 0)

    second = []
    for h in range(HALVES):
        left = panels_t[h * half : (h + 1) * half, :]
        for t in range(tiles):
            value = jnp.dot(left, high[t], preferred_element_type=jnp.float32)
            value += jnp.dot(left, low[t], preferred_element_type=jnp.float32)
            part[h, t] = value.astype(jnp.bfloat16)
        copies = []
        for j in far_first(n_dev):
            stage2[h, j] = part[h, found[j]]
            copy = pltpu.make_async_remote_copy(
                src_ref=stage2.at[h, j],
                dst_ref=got2.at[h, j],
                send_sem=send2.at[h, j],
                recv_sem=recv2.at[h, j],
                device_id=(g, lax.rem(d + j, n_dev)),
                device_id_type=MESH,
            )
            copy.start()
            copies.append(copy)
        got2[h, 0] = part[h, found[0]]
        second.append(copies)

    labels = []
    for j in range(n_dev):
        source = lax.rem(d + n_dev - j, n_dev)
        tag = fetched[source * piece + ncap * sub]
        labels.append(jnp.max(tag.astype(jnp.float32)))

    third = []
    step = 32
    for h in range(HALVES):
        for copy in second[h]:
            copy.wait()
        copies = []
        for jj in list(range(1, n_grp)) + [0]:
            target = lax.rem(g + jj, n_grp)
            weights = [
                [
                    jnp.where(labels[j] == (target * CT + q).astype(jnp.float32), 1.0, 0.0)
                    for j in range(n_dev)
                ]
                for q in range(CT)
            ]

            def add_up(r, unused):
                at = pl.ds(pl.multiple_of(r * step, step), step)
                sums = [jnp.zeros((step, W), jnp.float32) for q in range(CT)]
                for j in range(n_dev):
                    value = got2[h, j, at, :].astype(jnp.float32)
                    for q in range(CT):
                        sums[q] = sums[q] + value * weights[q][j]
                for q in range(CT):
                    if jj == 0:
                        mine[h, q, at, :] = sums[q]
                    else:
                        stage3[h, jj, q, at, :] = sums[q].astype(jnp.bfloat16)
                return unused

            lax.fori_loop(0, half // step, add_up, 0)
            if jj:
                copy = pltpu.make_async_remote_copy(
                    src_ref=stage3.at[h, jj],
                    dst_ref=got3.at[h, jj],
                    send_sem=send3.at[h, jj],
                    recv_sem=recv3.at[h, jj],
                    device_id=(target, d),
                    device_id_type=MESH,
                )
                copy.start()
                copies.append(copy)
        third.append(copies)

    for h in range(HALVES):
        for copy in third[h]:
            copy.wait()
        for q in range(CT):
            value = mine[h, q]
            for jj in range(1, n_grp):
                value = value + got3[h, jj, q].astype(jnp.float32)
            out_ref[q, h * half : (h + 1) * half, :] = value


def far_first(n):
    return sorted(range(1, n), key=lambda j: -min(j, n - j))


def body(blocks, prolong, block_cols, fetch_rows, tile_slot, tile_owner, tile_place):
    n_grp, n_dev = lax.axis_size("grp"), lax.axis_size("dev")
    rows = blocks.shape[2]
    slots = block_cols.shape[3]
    tiles = tile_owner.shape[2]
    ncap = fetch_rows.shape[3]
    if rows * tiles * BLOCK * slots * BLOCK * 2 > 16 * 2**20 or tiles > n_dev:
        return plain_body(
            blocks, prolong, block_cols, fetch_rows, tile_slot, tile_owner, tile_place
        )
    piece = ncap * (BLOCK // LABEL_ROWS) + 1
    half = W // HALVES
    vmem = pl.BlockSpec(memory_space=pltpu.VMEM)
    smem = pl.BlockSpec(memory_space=pltpu.SMEM)
    bf16, f32 = jnp.bfloat16, jnp.float32
    dma = pltpu.SemaphoreType.DMA
    result = pl.pallas_call(
        functools.partial(kernel, n_grp, n_dev),
        out_shape=jax.ShapeDtypeStruct((CT, W, W), f32),
        in_specs=[vmem, smem, smem, smem, smem, smem, pl.BlockSpec(memory_space=pl.ANY)],
        out_specs=vmem,
        scratch_shapes=[
            pltpu.VMEM((rows, BLOCK, slots * BLOCK), bf16),
            pltpu.VMEM((n_dev * piece, LABEL_ROWS, W), bf16),
            pltpu.VMEM((n_dev, piece, LABEL_ROWS, W), bf16),
            pltpu.VMEM((rows, tiles * BLOCK, slots * BLOCK), bf16),
            pltpu.VMEM((slots * BLOCK, W), bf16),
            pltpu.VMEM((tiles, rows * BLOCK, W), bf16),
            pltpu.VMEM((tiles, rows * BLOCK, W), bf16),
            pltpu.VMEM((W, rows * BLOCK), bf16),
            pltpu.VMEM((HALVES, tiles + 1, half, W), bf16),
            pltpu.VMEM((HALVES, n_dev, half, W), bf16),
            pltpu.VMEM((HALVES, n_dev, half, W), bf16),
            pltpu.VMEM((HALVES, n_grp, CT, half, W), bf16),
            pltpu.VMEM((HALVES, n_grp, CT, half, W), bf16),
            pltpu.VMEM((HALVES, CT, half, W), f32),
            dma,
            dma((n_dev,)),
            dma((n_dev,)),
            dma((HALVES, n_dev)),
            dma((HALVES, n_dev)),
            dma((HALVES, n_grp)),
            dma((HALVES, n_grp)),
        ],
        compiler_params=pltpu.CompilerParams(
            collective_id=0, has_side_effects=True, vmem_limit_bytes=48 * 2**20
        ),
    )(
        prolong[0, 0], block_cols[0, 0], fetch_rows[0, 0], tile_slot[0, 0], tile_owner[0, 0],
        tile_place[0, 0], blocks[0, 0],
    )
    return result.reshape(1, 1, CT, W, W)


def solution(mesh):
    return jax.shard_map(
        body,
        mesh=mesh,
        in_specs=(
            P("grp", "dev", None, None, None),
            P("grp", "dev", None, None, None),
            P("grp", "dev", None, None),
            P("grp", "dev", None, None),
            P("grp", "dev", None, None),
            P("grp", "dev", None),
            P("grp", "dev", None),
        ),
        out_specs=P("grp", "dev", None, None, None),
        check_vma=False,
    )
```

```python
import functools

import jax
import jax.numpy as jnp
from jax import lax
from jax.experimental import pallas as pl
from jax.experimental.pallas import tpu as pltpu
from jax.sharding import PartitionSpec as P

BLOCK = 64
W = 256
K = 27
CT = 2
NCAP = 3


def pick(panels, ids):
    ones = (ids[..., None] == jnp.arange(panels.shape[0], dtype=jnp.int32)).astype(panels.dtype)
    return jnp.einsum(
        "...p,prw->...rw", ones, panels, preferred_element_type=jnp.float32
    ).astype(panels.dtype)


def plain_body(blocks, prolong, block_cols, fetch_rows, tile_slot, tile_owner, tile_place):
    dev_count = lax.axis_size("dev")
    grp_count = lax.axis_size("grp")
    panels = prolong[0, 0]
    chosen = fetch_rows[0, 0]
    outgoing = pick(panels, chosen)
    arrived = lax.all_to_all(outgoing, "dev", split_axis=0, concat_axis=0, tiled=True)
    arrived = arrived.reshape(dev_count * NCAP, BLOCK, W)
    owners = tile_owner[0, 0]
    places = tile_place[0, 0]
    local_count = owners.shape[0]
    tile_range = jnp.arange(local_count, dtype=jnp.int32)

    def one_row(running, item):
        block_row, panel_row, column_ids, slot_ids = item
        matrix = block_row.reshape(BLOCK, K, BLOCK)
        near_panels = pick(arrived, column_ids)
        product = jnp.einsum(
            "rkc,kcw->krw", matrix, near_panels, preferred_element_type=jnp.float32
        )
        product = jnp.where((column_ids >= 0)[:, None, None], product, 0.0).astype(jnp.bfloat16)
        outer_tile = jnp.einsum(
            "ra,krb->kab", panel_row, product, preferred_element_type=jnp.float32
        )
        selector = (slot_ids[:, None] == tile_range[None, :]).astype(jnp.float32)
        added = jnp.einsum("kt,kab->tab", selector, outer_tile, precision=lax.Precision.HIGHEST)
        return (running + added, None)

    running = jnp.zeros((local_count, W, W), jnp.float32)
    running, unused = lax.scan(
        one_row, running, (blocks[0, 0], panels, block_cols[0, 0], tile_slot[0, 0])
    )
    partial_value = running.astype(jnp.bfloat16)
    dev_target = owners % dev_count
    grp_target = owners // dev_count
    sending = jnp.zeros((dev_count, W, W), jnp.bfloat16).at[dev_target].set(partial_value)
    labels = jnp.full((dev_count,), -1, jnp.int32).at[dev_target].set(grp_target * CT + places)
    got_tiles, got_labels = (
        lax.all_to_all(sending, "dev", split_axis=0, concat_axis=0, tiled=True),
        lax.all_to_all(labels, "dev", split_axis=0, concat_axis=0, tiled=True),
    )
    spread = grp_count * CT
    keyed = jnp.where(got_labels >= 0, got_labels, spread)
    table = (
        jnp.zeros((spread, W, W), jnp.float32)
        .at[keyed]
        .add(got_tiles.astype(jnp.float32), mode="drop")
    )
    result = lax.psum_scatter(table, "grp", scatter_dimension=0, tiled=True)
    return result.reshape(1, 1, CT, W, W)


MESH = pl.DeviceIdType.MESH
HALVES = 2
CUTS = 2
LABEL_ROWS = 16


def kernel(
    n_grp, n_dev, cols_ref, fetch_ref, slot_ref, owner_ref, place_ref, prolong_hbm, blocks_hbm,
    out_ref,
    prolong_ref, mat, fetched_a, fetched_b, stage1, spread, near, high, low, panels_t, part, stage2, got2,
    stage3, got3, mine,
    prolong_sem, blocks_sem, send1, recv1, send2, recv2, send3, recv3,
):
    rows = blocks_hbm.shape[0]
    slots = cols_ref.shape[2]
    tiles = owner_ref.shape[0]
    ncap = fetch_ref.shape[0]
    sub = BLOCK // LABEL_ROWS
    piece = ncap * sub + 1
    wide = W // HALVES
    tall = W // CUTS
    g = lax.axis_index("grp")
    d = lax.axis_index("dev")
    fetched = (fetched_a, fetched_b)
    first_load = pltpu.make_async_copy(prolong_hbm, prolong_ref, prolong_sem)
    first_load.start()
    load = pltpu.make_async_copy(blocks_hbm, mat, blocks_sem)
    load.start()

    barrier = pltpu.get_barrier_semaphore()
    for j in range(1, n_dev):
        pl.semaphore_signal(barrier, inc=1, device_id=(g, lax.rem(d + j, n_dev)), device_id_type=MESH)
    for j in range(1, n_grp):
        pl.semaphore_signal(barrier, inc=1, device_id=(lax.rem(g + j, n_grp), d), device_id_type=MESH)

    def tile_for(target):
        found = jnp.int32(tiles)
        label = jnp.int32(-1)
        for t in range(tiles):
            hit = lax.rem(owner_ref[t], n_dev) == target
            found = jnp.where(hit, t, found)
            label = jnp.where(hit, lax.div(owner_ref[t], n_dev) * CT + place_ref[t], label)
        return found, label

    def fill(where, target, base, label):
        tag = jnp.full((1, LABEL_ROWS, wide), label.astype(jnp.float32), jnp.float32)
        tag = tag.astype(jnp.bfloat16)
        for c in range(ncap):
            panel = prolong_ref[fetch_ref[c, 0, target]]
            for h in range(HALVES):
                half = panel[:, h * wide : (h + 1) * wide]
                where[h][pl.ds(base + c * sub, sub)] = half.reshape(sub, LABEL_ROWS, wide)
        for h in range(HALVES):
            where[h][pl.ds(base + ncap * sub, 1)] = tag

    first_load.wait()
    found = [None] * n_dev
    labels = [None] * n_dev
    for j in range(n_dev):
        found[j], labels[j] = tile_for(lax.rem(d + j, n_dev))
    first = [[] for h in range(HALVES)]
    order = far_first(n_dev)

    def send_panels(h, j):
        copy = pltpu.make_async_remote_copy(
            src_ref=stage1.at[j, h],
            dst_ref=fetched[h].at[pl.ds(d * piece, piece)],
            send_sem=send1.at[h, j],
            recv_sem=recv1.at[h, j],
            device_id=(g, lax.rem(d + j, n_dev)),
            device_id_type=MESH,
        )
        copy.start()
        first[h].append(copy)

    for j in order:
        fill([stage1.at[j, h] for h in range(HALVES)], lax.rem(d + j, n_dev), 0, labels[j])
        if j == order[0]:
            pl.semaphore_wait(barrier, n_dev - 1 + n_grp - 1)
        send_panels(0, j)
    for h in range(1, HALVES):
        for j in order:
            send_panels(h, j)
    fill(fetched, d, d * piece, labels[0])

    panels_t[...] = prolong_ref[...].reshape(rows * BLOCK, W).T
    for h in range(HALVES):
        part[h, tiles] = jnp.zeros((W, wide), jnp.bfloat16)
    load.wait()
    lane = lax.broadcasted_iota(jnp.int32, (1, 2 * BLOCK), 1)

    def place_blocks(i, unused):
        for k in range(0, slots, 2):
            width = min(2, slots - k) * BLOCK
            ids = [
                jnp.where(cols_ref[i, 0, m] >= 0, slot_ref[i, 0, m], -1)
                for m in range(k, min(k + 2, slots))
            ]
            ids = jnp.where(lane < BLOCK, ids[0], ids[-1])[:, :width]
            at = slice(k * BLOCK, k * BLOCK + width)
            values = mat[i, :, at]
            for t in range(tiles):
                mask = jnp.where(ids == t, 1.0, 0.0).astype(jnp.bfloat16)
                spread[i, t * BLOCK : (t + 1) * BLOCK, at] = values * mask
        return unused

    lax.fori_loop(0, rows, place_blocks, 0)

    second = []
    for h in range(HALVES):
        for copy in first[h]:
            copy.wait()

        def one_row(i, unused):
            for k in range(slots):
                col = jnp.maximum(cols_ref[i, 0, k], 0)
                panel = fetched[h][pl.ds(col * sub + lax.div(col, ncap), sub)]
                near[k * BLOCK : (k + 1) * BLOCK, :] = panel.reshape(BLOCK, wide)
            total = jnp.dot(spread[i], near[...], preferred_element_type=jnp.float32)
            top = total.astype(jnp.bfloat16)
            rest = (total - top.astype(jnp.float32)).astype(jnp.bfloat16)
            at = pl.ds(pl.multiple_of(i * BLOCK, BLOCK), BLOCK)
            for t in range(tiles):
                mine_at = slice(t * wide, (t + 1) * wide)
                high[at, mine_at] = top[t * BLOCK : (t + 1) * BLOCK]
                low[at, mine_at] = rest[t * BLOCK : (t + 1) * BLOCK]
            return unused

        lax.fori_loop(0, rows, one_row, 0)

        for v in range(CUTS):
            down = slice(v * tall, (v + 1) * tall)
            left = panels_t[down, :]
            value = jnp.dot(left, high[...], preferred_element_type=jnp.float32)
            value += jnp.dot(left, low[...], preferred_element_type=jnp.float32)
            for t in range(tiles):
                part[h, t, down, :] = value[:, t * wide : (t + 1) * wide].astype(jnp.bfloat16)
            copies = []
            for j in order:
                stage2[h, v, j] = part[h, found[j], down, :]
                copy = pltpu.make_async_remote_copy(
                    src_ref=stage2.at[h, v, j],
                    dst_ref=got2.at[h, v, j],
                    send_sem=send2.at[h, v, j],
                    recv_sem=recv2.at[h, v, j],
                    device_id=(g, lax.rem(d + j, n_dev)),
                    device_id_type=MESH,
                )
                copy.start()
                copies.append(copy)
            got2[h, v, 0] = part[h, found[0], down, :]
            second.append(copies)

    marks = []
    for j in range(n_dev):
        source = lax.rem(d + n_dev - j, n_dev)
        tag = fetched[0][source * piece + ncap * sub]
        marks.append(jnp.max(tag.astype(jnp.float32)))

    third = []
    step = 32
    for n in range(HALVES * CUTS):
        h, v = n // CUTS, n % CUTS
        for copy in second[n]:
            copy.wait()
        copies = []
        for jj in list(range(1, n_grp)) + [0]:
            target = lax.rem(g + jj, n_grp)
            weights = [
                [
                    jnp.where(marks[j] == (target * CT + q).astype(jnp.float32), 1.0, 0.0)
                    for j in range(n_dev)
                ]
                for q in range(CT)
            ]

            def add_up(r, unused):
                at = pl.ds(pl.multiple_of(r * step, step), step)
                sums = [jnp.zeros((step, wide), jnp.float32) for q in range(CT)]
                for j in range(n_dev):
                    value = got2[h, v, j, at, :].astype(jnp.float32)
                    for q in range(CT):
                        sums[q] = sums[q] + value * weights[q][j]
                for q in range(CT):
                    if jj == 0:
                        mine[h, v, q, at, :] = sums[q]
                    else:
                        stage3[h, v, jj, q, at, :] = sums[q].astype(jnp.bfloat16)
                return unused

            lax.fori_loop(0, tall // step, add_up, 0)
            if jj:
                copy = pltpu.make_async_remote_copy(
                    src_ref=stage3.at[h, v, jj],
                    dst_ref=got3.at[h, v, jj],
                    send_sem=send3.at[h, v, jj],
                    recv_sem=recv3.at[h, v, jj],
                    device_id=(target, d),
                    device_id_type=MESH,
                )
                copy.start()
                copies.append(copy)
        third.append(copies)

    for n in range(HALVES * CUTS):
        h, v = n // CUTS, n % CUTS
        for copy in third[n]:
            copy.wait()
        for q in range(CT):
            value = mine[h, v, q]
            for jj in range(1, n_grp):
                value = value + got3[h, v, jj, q].astype(jnp.float32)
            out_ref[q, v * tall : (v + 1) * tall, h * wide : (h + 1) * wide] = value


def far_first(n):
    return sorted(range(1, n), key=lambda j: -min(j, n - j))


def body(blocks, prolong, block_cols, fetch_rows, tile_slot, tile_owner, tile_place):
    n_grp, n_dev = lax.axis_size("grp"), lax.axis_size("dev")
    rows = blocks.shape[2]
    slots = block_cols.shape[3]
    tiles = tile_owner.shape[2]
    ncap = fetch_rows.shape[3]
    if rows * tiles * BLOCK * slots * BLOCK * 2 > 16 * 2**20 or tiles > n_dev:
        return plain_body(
            blocks, prolong, block_cols, fetch_rows, tile_slot, tile_owner, tile_place
        )
    piece = ncap * (BLOCK // LABEL_ROWS) + 1
    wide, tall = W // HALVES, W // CUTS
    vmem = pl.BlockSpec(memory_space=pltpu.VMEM)
    smem = pl.BlockSpec(memory_space=pltpu.SMEM)
    bf16, f32 = jnp.bfloat16, jnp.float32
    dma = pltpu.SemaphoreType.DMA
    result = pl.pallas_call(
        functools.partial(kernel, n_grp, n_dev),
        out_shape=jax.ShapeDtypeStruct((CT, W, W), f32),
        in_specs=[smem] * 5 + [pl.BlockSpec(memory_space=pltpu.HBM)] * 2,
        out_specs=vmem,
        scratch_shapes=[
            pltpu.VMEM((rows, BLOCK, W), bf16),
            pltpu.VMEM((rows, BLOCK, slots * BLOCK), bf16),
            pltpu.VMEM((n_dev * piece, LABEL_ROWS, wide), bf16),
            pltpu.VMEM((n_dev * piece, LABEL_ROWS, wide), bf16),
            pltpu.VMEM((n_dev, HALVES, piece, LABEL_ROWS, wide), bf16),
            pltpu.VMEM((rows, tiles * BLOCK, slots * BLOCK), bf16),
            pltpu.VMEM((slots * BLOCK, wide), bf16),
            pltpu.VMEM((rows * BLOCK, tiles * wide), bf16),
            pltpu.VMEM((rows * BLOCK, tiles * wide), bf16),
            pltpu.VMEM((W, rows * BLOCK), bf16),
            pltpu.VMEM((HALVES, tiles + 1, W, wide), bf16),
            pltpu.VMEM((HALVES, CUTS, n_dev, tall, wide), bf16),
            pltpu.VMEM((HALVES, CUTS, n_dev, tall, wide), bf16),
            pltpu.VMEM((HALVES, CUTS, n_grp, CT, tall, wide), bf16),
            pltpu.VMEM((HALVES, CUTS, n_grp, CT, tall, wide), bf16),
            pltpu.VMEM((HALVES, CUTS, CT, tall, wide), f32),
            dma,
            dma,
            dma((HALVES, n_dev)),
            dma((HALVES, n_dev)),
            dma((HALVES, CUTS, n_dev)),
            dma((HALVES, CUTS, n_dev)),
            dma((HALVES, CUTS, n_grp)),
            dma((HALVES, CUTS, n_grp)),
        ],
        compiler_params=pltpu.CompilerParams(
            collective_id=0, has_side_effects=True, vmem_limit_bytes=62 * 2**20
        ),
    )(
        block_cols[0].transpose(1, 0, 2), fetch_rows[0].transpose(2, 0, 1), tile_slot[0].transpose(1, 0, 2),
        tile_owner[0, 0], tile_place[0, 0], prolong[0, 0], blocks[0, 0],
    )
    return result.reshape(1, 1, CT, W, W)


def solution(mesh):
    return jax.shard_map(
        body,
        mesh=mesh,
        in_specs=(
            P("grp", "dev", None, None, None),
            P("grp", "dev", None, None, None),
            P("grp", "dev", None, None),
            P("grp", "dev", None, None),
            P("grp", "dev", None, None),
            P("grp", "dev", None),
            P("grp", "dev", None),
        ),
        out_specs=P("grp", "dev", None, None, None),
        check_vma=False,
    )
```

```python
import functools

import jax
import jax.numpy as jnp
from jax import lax
from jax.experimental import pallas as pl
from jax.experimental.pallas import tpu as pltpu
from jax.sharding import PartitionSpec as P

BLOCK = 64
W = 256
K = 27
CT = 2
NCAP = 3


def pick(panels, ids):
    ones = (ids[..., None] == jnp.arange(panels.shape[0], dtype=jnp.int32)).astype(panels.dtype)
    return jnp.einsum(
        "...p,prw->...rw", ones, panels, preferred_element_type=jnp.float32
    ).astype(panels.dtype)


def plain_body(blocks, prolong, block_cols, fetch_rows, tile_slot, tile_owner, tile_place):
    dev_count = lax.axis_size("dev")
    grp_count = lax.axis_size("grp")
    panels = prolong[0, 0]
    chosen = fetch_rows[0, 0]
    outgoing = pick(panels, chosen)
    arrived = lax.all_to_all(outgoing, "dev", split_axis=0, concat_axis=0, tiled=True)
    arrived = arrived.reshape(dev_count * NCAP, BLOCK, W)
    owners = tile_owner[0, 0]
    places = tile_place[0, 0]
    local_count = owners.shape[0]
    tile_range = jnp.arange(local_count, dtype=jnp.int32)

    def one_row(running, item):
        block_row, panel_row, column_ids, slot_ids = item
        matrix = block_row.reshape(BLOCK, K, BLOCK)
        near_panels = pick(arrived, column_ids)
        product = jnp.einsum(
            "rkc,kcw->krw", matrix, near_panels, preferred_element_type=jnp.float32
        )
        product = jnp.where((column_ids >= 0)[:, None, None], product, 0.0).astype(jnp.bfloat16)
        outer_tile = jnp.einsum(
            "ra,krb->kab", panel_row, product, preferred_element_type=jnp.float32
        )
        selector = (slot_ids[:, None] == tile_range[None, :]).astype(jnp.float32)
        added = jnp.einsum("kt,kab->tab", selector, outer_tile, precision=lax.Precision.HIGHEST)
        return (running + added, None)

    running = jnp.zeros((local_count, W, W), jnp.float32)
    running, unused = lax.scan(
        one_row, running, (blocks[0, 0], panels, block_cols[0, 0], tile_slot[0, 0])
    )
    partial_value = running.astype(jnp.bfloat16)
    dev_target = owners % dev_count
    grp_target = owners // dev_count
    sending = jnp.zeros((dev_count, W, W), jnp.bfloat16).at[dev_target].set(partial_value)
    labels = jnp.full((dev_count,), -1, jnp.int32).at[dev_target].set(grp_target * CT + places)
    got_tiles, got_labels = (
        lax.all_to_all(sending, "dev", split_axis=0, concat_axis=0, tiled=True),
        lax.all_to_all(labels, "dev", split_axis=0, concat_axis=0, tiled=True),
    )
    spread = grp_count * CT
    keyed = jnp.where(got_labels >= 0, got_labels, spread)
    table = (
        jnp.zeros((spread, W, W), jnp.float32)
        .at[keyed]
        .add(got_tiles.astype(jnp.float32), mode="drop")
    )
    result = lax.psum_scatter(table, "grp", scatter_dimension=0, tiled=True)
    return result.reshape(1, 1, CT, W, W)


MESH = pl.DeviceIdType.MESH
HALVES = 2
CUTS = 2
LABEL_ROWS = 16


def kernel(
    n_grp, n_dev, cols_hbm, fetch_hbm, slot_hbm, owner_hbm, place_hbm, prolong_hbm, blocks_hbm,
    out_hbm,
    cols_ref, fetch_ref, slot_ref, owner_ref, place_ref, out_ref,
    prolong_ref, mat, fetched_a, fetched_b, stage1, spread, near, high, low, panels_t, part, stage2, got2,
    stage3, got3, mine,
    prolong_sem, blocks_sem, ids_sem, out_sem, send1, recv1, send2, recv2, send3, recv3,
):
    rows = blocks_hbm.shape[0]
    slots = cols_ref.shape[2]
    tiles = owner_ref.shape[0]
    ncap = fetch_ref.shape[0]
    sub = BLOCK // LABEL_ROWS
    piece = ncap * sub + 1
    wide = W // HALVES
    tall = W // CUTS
    g = lax.axis_index("grp")
    d = lax.axis_index("dev")
    fetched = (fetched_a, fetched_b)
    id_loads = [
        pltpu.make_async_copy(source, target, ids_sem.at[n])
        for n, (source, target) in enumerate(
            (
                (fetch_hbm, fetch_ref), (owner_hbm, owner_ref), (place_hbm, place_ref),
                (cols_hbm, cols_ref), (slot_hbm, slot_ref),
            )
        )
    ]
    for copy in id_loads:
        copy.start()
    first_load = pltpu.make_async_copy(prolong_hbm, prolong_ref, prolong_sem)
    first_load.start()
    load = pltpu.make_async_copy(blocks_hbm, mat, blocks_sem)
    load.start()

    barrier = pltpu.get_barrier_semaphore()
    for j in range(1, n_dev):
        pl.semaphore_signal(barrier, inc=1, device_id=(g, lax.rem(d + j, n_dev)), device_id_type=MESH)
    for j in range(1, n_grp):
        pl.semaphore_signal(barrier, inc=1, device_id=(lax.rem(g + j, n_grp), d), device_id_type=MESH)

    def tile_for(target):
        found = jnp.int32(tiles)
        label = jnp.int32(-1)
        for t in range(tiles):
            hit = lax.rem(owner_ref[t], n_dev) == target
            found = jnp.where(hit, t, found)
            label = jnp.where(hit, lax.div(owner_ref[t], n_dev) * CT + place_ref[t], label)
        return found, label

    def fill(where, target, base, label):
        tag = jnp.full((1, LABEL_ROWS, wide), label.astype(jnp.float32), jnp.float32)
        tag = tag.astype(jnp.bfloat16)
        for c in range(ncap):
            panel = prolong_ref[fetch_ref[c, 0, target]]
            for h in range(HALVES):
                half = panel[:, h * wide : (h + 1) * wide]
                where[h][pl.ds(base + c * sub, sub)] = half.reshape(sub, LABEL_ROWS, wide)
        for h in range(HALVES):
            where[h][pl.ds(base + ncap * sub, 1)] = tag

    for copy in id_loads:
        copy.wait()
    first_load.wait()
    found = [None] * n_dev
    labels = [None] * n_dev
    for j in range(n_dev):
        found[j], labels[j] = tile_for(lax.rem(d + j, n_dev))
    first = [[] for h in range(HALVES)]
    order = far_first(n_dev)

    def send_panels(h, j):
        copy = pltpu.make_async_remote_copy(
            src_ref=stage1.at[j, h],
            dst_ref=fetched[h].at[pl.ds(d * piece, piece)],
            send_sem=send1.at[h, j],
            recv_sem=recv1.at[h, j],
            device_id=(g, lax.rem(d + j, n_dev)),
            device_id_type=MESH,
        )
        copy.start()
        first[h].append(copy)

    for j in order:
        fill([stage1.at[j, h] for h in range(HALVES)], lax.rem(d + j, n_dev), 0, labels[j])
        if j == order[0]:
            pl.semaphore_wait(barrier, n_dev - 1 + n_grp - 1)
        send_panels(0, j)
    for h in range(1, HALVES):
        for j in order:
            send_panels(h, j)
    fill(fetched, d, d * piece, labels[0])

    panels_t[...] = prolong_ref[...].reshape(rows * BLOCK, W).T
    for h in range(HALVES):
        part[h, tiles] = jnp.zeros((W, wide), jnp.bfloat16)
    load.wait()
    lane = lax.broadcasted_iota(jnp.int32, (1, 2 * BLOCK), 1)

    def place_blocks(i, unused):
        for k in range(0, slots, 2):
            width = min(2, slots - k) * BLOCK
            ids = [
                jnp.where(cols_ref[i, 0, m] >= 0, slot_ref[i, 0, m], -1)
                for m in range(k, min(k + 2, slots))
            ]
            ids = jnp.where(lane < BLOCK, ids[0], ids[-1])[:, :width]
            at = slice(k * BLOCK, k * BLOCK + width)
            values = mat[i, :, at]
            for t in range(tiles):
                mask = jnp.where(ids == t, 1.0, 0.0).astype(jnp.bfloat16)
                spread[i, t * BLOCK : (t + 1) * BLOCK, at] = values * mask
        return unused

    lax.fori_loop(0, rows, place_blocks, 0)

    second = []
    for h in range(HALVES):
        for copy in first[h]:
            copy.wait()

        def one_row(i, unused):
            for k in range(slots):
                col = jnp.maximum(cols_ref[i, 0, k], 0)
                panel = fetched[h][pl.ds(col * sub + lax.div(col, ncap), sub)]
                near[k * BLOCK : (k + 1) * BLOCK, :] = panel.reshape(BLOCK, wide)
            total = jnp.dot(spread[i], near[...], preferred_element_type=jnp.float32)
            top = total.astype(jnp.bfloat16)
            rest = (total - top.astype(jnp.float32)).astype(jnp.bfloat16)
            at = pl.ds(pl.multiple_of(i * BLOCK, BLOCK), BLOCK)
            for t in range(tiles):
                mine_at = slice(t * wide, (t + 1) * wide)
                high[at, mine_at] = top[t * BLOCK : (t + 1) * BLOCK]
                low[at, mine_at] = rest[t * BLOCK : (t + 1) * BLOCK]
            return unused

        lax.fori_loop(0, rows, one_row, 0)

        for v in range(CUTS):
            down = slice(v * tall, (v + 1) * tall)
            left = panels_t[down, :]
            value = jnp.dot(left, high[...], preferred_element_type=jnp.float32)
            value += jnp.dot(left, low[...], preferred_element_type=jnp.float32)
            for t in range(tiles):
                part[h, t, down, :] = value[:, t * wide : (t + 1) * wide].astype(jnp.bfloat16)
            copies = []
            for j in order:
                stage2[h, v, j] = part[h, found[j], down, :]
                copy = pltpu.make_async_remote_copy(
                    src_ref=stage2.at[h, v, j],
                    dst_ref=got2.at[h, v, j],
                    send_sem=send2.at[h, v, j],
                    recv_sem=recv2.at[h, v, j],
                    device_id=(g, lax.rem(d + j, n_dev)),
                    device_id_type=MESH,
                )
                copy.start()
                copies.append(copy)
            got2[h, v, 0] = part[h, found[0], down, :]
            second.append(copies)

    marks = []
    for j in range(n_dev):
        source = lax.rem(d + n_dev - j, n_dev)
        tag = fetched[0][source * piece + ncap * sub]
        marks.append(jnp.max(tag.astype(jnp.float32)))

    third = []
    step = 32
    for n in range(HALVES * CUTS):
        h, v = n // CUTS, n % CUTS
        for copy in second[n]:
            copy.wait()
        copies = []
        for jj in list(range(1, n_grp)) + [0]:
            target = lax.rem(g + jj, n_grp)
            weights = [
                [
                    jnp.where(marks[j] == (target * CT + q).astype(jnp.float32), 1.0, 0.0)
                    for j in range(n_dev)
                ]
                for q in range(CT)
            ]

            def add_up(r, unused):
                at = pl.ds(pl.multiple_of(r * step, step), step)
                sums = [jnp.zeros((step, wide), jnp.float32) for q in range(CT)]
                for j in range(n_dev):
                    value = got2[h, v, j, at, :].astype(jnp.float32)
                    for q in range(CT):
                        sums[q] = sums[q] + value * weights[q][j]
                for q in range(CT):
                    if jj == 0:
                        mine[h, v, q, at, :] = sums[q]
                    else:
                        stage3[h, v, jj, q, at, :] = sums[q].astype(jnp.bfloat16)
                return unused

            lax.fori_loop(0, tall // step, add_up, 0)
            if jj:
                copy = pltpu.make_async_remote_copy(
                    src_ref=stage3.at[h, v, jj],
                    dst_ref=got3.at[h, v, jj],
                    send_sem=send3.at[h, v, jj],
                    recv_sem=recv3.at[h, v, jj],
                    device_id=(target, d),
                    device_id_type=MESH,
                )
                copy.start()
                copies.append(copy)
        third.append(copies)

    saves = []
    for n in range(HALVES * CUTS):
        h, v = n // CUTS, n % CUTS
        for copy in third[n]:
            copy.wait()
        for q in range(CT):
            value = mine[h, v, q]
            for jj in range(1, n_grp):
                value = value + got3[h, v, jj, q].astype(jnp.float32)
            out_ref[n, q] = value
        save = pltpu.make_async_copy(
            out_ref.at[n],
            out_hbm.at[:, pl.ds(v * tall, tall), pl.ds(h * wide, wide)],
            out_sem.at[n],
        )
        save.start()
        saves.append(save)
    for save in saves:
        save.wait()


def far_first(n):
    return sorted(range(1, n), key=lambda j: -min(j, n - j))


def body(blocks, prolong, block_cols, fetch_rows, tile_slot, tile_owner, tile_place):
    n_grp, n_dev = lax.axis_size("grp"), lax.axis_size("dev")
    rows = blocks.shape[2]
    slots = block_cols.shape[3]
    tiles = tile_owner.shape[2]
    ncap = fetch_rows.shape[3]
    if rows * tiles * BLOCK * slots * BLOCK * 2 > 16 * 2**20 or tiles > n_dev:
        return plain_body(
            blocks, prolong, block_cols, fetch_rows, tile_slot, tile_owner, tile_place
        )
    piece = ncap * (BLOCK // LABEL_ROWS) + 1
    wide, tall = W // HALVES, W // CUTS
    bf16, f32 = jnp.bfloat16, jnp.float32
    dma = pltpu.SemaphoreType.DMA
    result = pl.pallas_call(
        functools.partial(kernel, n_grp, n_dev),
        out_shape=jax.ShapeDtypeStruct((CT, W, W), f32),
        in_specs=[pl.BlockSpec(memory_space=pl.ANY)] * 7,
        out_specs=pl.BlockSpec(memory_space=pl.ANY),
        scratch_shapes=[
            pltpu.SMEM((rows, 1, slots), jnp.int32),
            pltpu.SMEM((ncap, 1, n_dev), jnp.int32),
            pltpu.SMEM((rows, 1, slots), jnp.int32),
            pltpu.SMEM((tiles,), jnp.int32),
            pltpu.SMEM((tiles,), jnp.int32),
            pltpu.VMEM((HALVES * CUTS, CT, tall, wide), f32),
            pltpu.VMEM((rows, BLOCK, W), bf16),
            pltpu.VMEM((rows, BLOCK, slots * BLOCK), bf16),
            pltpu.VMEM((n_dev * piece, LABEL_ROWS, wide), bf16),
            pltpu.VMEM((n_dev * piece, LABEL_ROWS, wide), bf16),
            pltpu.VMEM((n_dev, HALVES, piece, LABEL_ROWS, wide), bf16),
            pltpu.VMEM((rows, tiles * BLOCK, slots * BLOCK), bf16),
            pltpu.VMEM((slots * BLOCK, wide), bf16),
            pltpu.VMEM((rows * BLOCK, tiles * wide), bf16),
            pltpu.VMEM((rows * BLOCK, tiles * wide), bf16),
            pltpu.VMEM((W, rows * BLOCK), bf16),
            pltpu.VMEM((HALVES, tiles + 1, W, wide), bf16),
            pltpu.VMEM((HALVES, CUTS, n_dev, tall, wide), bf16),
            pltpu.VMEM((HALVES, CUTS, n_dev, tall, wide), bf16),
            pltpu.VMEM((HALVES, CUTS, n_grp, CT, tall, wide), bf16),
            pltpu.VMEM((HALVES, CUTS, n_grp, CT, tall, wide), bf16),
            pltpu.VMEM((HALVES, CUTS, CT, tall, wide), f32),
            dma,
            dma,
            dma((5,)),
            dma((HALVES * CUTS,)),
            dma((HALVES, n_dev)),
            dma((HALVES, n_dev)),
            dma((HALVES, CUTS, n_dev)),
            dma((HALVES, CUTS, n_dev)),
            dma((HALVES, CUTS, n_grp)),
            dma((HALVES, CUTS, n_grp)),
        ],
        compiler_params=pltpu.CompilerParams(
            collective_id=0, has_side_effects=True, vmem_limit_bytes=62 * 2**20
        ),
    )(
        block_cols[0].transpose(1, 0, 2), fetch_rows[0].transpose(2, 0, 1), tile_slot[0].transpose(1, 0, 2),
        tile_owner[0, 0], tile_place[0, 0], prolong[0, 0], blocks[0, 0],
    )
    return result.reshape(1, 1, CT, W, W)


def solution(mesh):
    return jax.shard_map(
        body,
        mesh=mesh,
        in_specs=(
            P("grp", "dev", None, None, None),
            P("grp", "dev", None, None, None),
            P("grp", "dev", None, None),
            P("grp", "dev", None, None),
            P("grp", "dev", None, None),
            P("grp", "dev", None),
            P("grp", "dev", None),
        ),
        out_specs=P("grp", "dev", None, None, None),
        check_vma=False,
    )
```

```python
import functools

import jax
import jax.numpy as jnp
from jax import lax
from jax.experimental import pallas as pl
from jax.experimental.pallas import tpu as pltpu
from jax.sharding import PartitionSpec as P

BLOCK = 64
W = 256
K = 27
CT = 2
NCAP = 3


def pick(panels, ids):
    ones = (ids[..., None] == jnp.arange(panels.shape[0], dtype=jnp.int32)).astype(panels.dtype)
    return jnp.einsum(
        "...p,prw->...rw", ones, panels, preferred_element_type=jnp.float32
    ).astype(panels.dtype)


def plain_body(blocks, prolong, block_cols, fetch_rows, tile_slot, tile_owner, tile_place):
    dev_count = lax.axis_size("dev")
    grp_count = lax.axis_size("grp")
    panels = prolong[0, 0]
    chosen = fetch_rows[0, 0]
    outgoing = pick(panels, chosen)
    arrived = lax.all_to_all(outgoing, "dev", split_axis=0, concat_axis=0, tiled=True)
    arrived = arrived.reshape(dev_count * NCAP, BLOCK, W)
    owners = tile_owner[0, 0]
    places = tile_place[0, 0]
    local_count = owners.shape[0]
    tile_range = jnp.arange(local_count, dtype=jnp.int32)

    def one_row(running, item):
        block_row, panel_row, column_ids, slot_ids = item
        matrix = block_row.reshape(BLOCK, K, BLOCK)
        near_panels = pick(arrived, column_ids)
        product = jnp.einsum(
            "rkc,kcw->krw", matrix, near_panels, preferred_element_type=jnp.float32
        )
        product = jnp.where((column_ids >= 0)[:, None, None], product, 0.0).astype(jnp.bfloat16)
        outer_tile = jnp.einsum(
            "ra,krb->kab", panel_row, product, preferred_element_type=jnp.float32
        )
        selector = (slot_ids[:, None] == tile_range[None, :]).astype(jnp.float32)
        added = jnp.einsum("kt,kab->tab", selector, outer_tile, precision=lax.Precision.HIGHEST)
        return (running + added, None)

    running = jnp.zeros((local_count, W, W), jnp.float32)
    running, unused = lax.scan(
        one_row, running, (blocks[0, 0], panels, block_cols[0, 0], tile_slot[0, 0])
    )
    partial_value = running.astype(jnp.bfloat16)
    dev_target = owners % dev_count
    grp_target = owners // dev_count
    sending = jnp.zeros((dev_count, W, W), jnp.bfloat16).at[dev_target].set(partial_value)
    labels = jnp.full((dev_count,), -1, jnp.int32).at[dev_target].set(grp_target * CT + places)
    got_tiles, got_labels = (
        lax.all_to_all(sending, "dev", split_axis=0, concat_axis=0, tiled=True),
        lax.all_to_all(labels, "dev", split_axis=0, concat_axis=0, tiled=True),
    )
    spread = grp_count * CT
    keyed = jnp.where(got_labels >= 0, got_labels, spread)
    table = (
        jnp.zeros((spread, W, W), jnp.float32)
        .at[keyed]
        .add(got_tiles.astype(jnp.float32), mode="drop")
    )
    result = lax.psum_scatter(table, "grp", scatter_dimension=0, tiled=True)
    return result.reshape(1, 1, CT, W, W)


MESH = pl.DeviceIdType.MESH
HALVES = 2
CUTS = 4
LABEL_ROWS = 16


def kernel(
    n_grp, n_dev, cols_hbm, fetch_hbm, slot_hbm, owner_hbm, place_hbm, prolong_hbm, blocks_hbm,
    out_hbm,
    cols_ref, fetch_ref, slot_ref, owner_ref, place_ref, out_ref,
    prolong_ref, mat, fetched_a, fetched_b, stage1, spread, near, high, low, panels_t, part, stage2, got2,
    stage3, got3, mine,
    prolong_sem, blocks_sem, ids_sem, out_sem, send1, recv1, send2, recv2, send3, recv3,
):
    rows = blocks_hbm.shape[0]
    slots = cols_ref.shape[2]
    tiles = owner_ref.shape[0]
    ncap = fetch_ref.shape[0]
    sub = BLOCK // LABEL_ROWS
    piece = ncap * sub + 1
    wide = W // HALVES
    tall = W // CUTS
    g = lax.axis_index("grp")
    d = lax.axis_index("dev")
    fetched = (fetched_a, fetched_b)
    id_loads = [
        pltpu.make_async_copy(source, target, ids_sem.at[n])
        for n, (source, target) in enumerate(
            (
                (fetch_hbm, fetch_ref), (owner_hbm, owner_ref), (place_hbm, place_ref),
                (cols_hbm, cols_ref), (slot_hbm, slot_ref),
            )
        )
    ]
    for copy in id_loads:
        copy.start()
    first_load = pltpu.make_async_copy(prolong_hbm, prolong_ref, prolong_sem)
    first_load.start()
    load = pltpu.make_async_copy(blocks_hbm, mat, blocks_sem)
    load.start()

    barrier = pltpu.get_barrier_semaphore()
    for j in range(1, n_dev):
        pl.semaphore_signal(barrier, inc=1, device_id=(g, lax.rem(d + j, n_dev)), device_id_type=MESH)
    for j in range(1, n_grp):
        pl.semaphore_signal(barrier, inc=1, device_id=(lax.rem(g + j, n_grp), d), device_id_type=MESH)

    def tile_for(target):
        found = jnp.int32(tiles)
        label = jnp.int32(-1)
        for t in range(tiles):
            hit = lax.rem(owner_ref[t], n_dev) == target
            found = jnp.where(hit, t, found)
            label = jnp.where(hit, lax.div(owner_ref[t], n_dev) * CT + place_ref[t], label)
        return found, label

    def fill(where, target, base, label):
        tag = jnp.full((1, LABEL_ROWS, wide), label.astype(jnp.float32), jnp.float32)
        tag = tag.astype(jnp.bfloat16)
        for c in range(ncap):
            panel = prolong_ref[fetch_ref[c, 0, target]]
            for h in range(HALVES):
                half = panel[:, h * wide : (h + 1) * wide]
                where[h][pl.ds(base + c * sub, sub)] = half.reshape(sub, LABEL_ROWS, wide)
        for h in range(HALVES):
            where[h][pl.ds(base + ncap * sub, 1)] = tag

    for copy in id_loads:
        copy.wait()
    first_load.wait()
    found = [None] * n_dev
    labels = [None] * n_dev
    for j in range(n_dev):
        found[j], labels[j] = tile_for(lax.rem(d + j, n_dev))
    first = [[] for h in range(HALVES)]
    order = far_first(n_dev)

    def send_panels(h, j):
        copy = pltpu.make_async_remote_copy(
            src_ref=stage1.at[j, h],
            dst_ref=fetched[h].at[pl.ds(d * piece, piece)],
            send_sem=send1.at[h, j],
            recv_sem=recv1.at[h, j],
            device_id=(g, lax.rem(d + j, n_dev)),
            device_id_type=MESH,
        )
        copy.start()
        first[h].append(copy)

    for j in order:
        fill([stage1.at[j, h] for h in range(HALVES)], lax.rem(d + j, n_dev), 0, labels[j])
        if j == order[0]:
            pl.semaphore_wait(barrier, n_dev - 1 + n_grp - 1)
        send_panels(0, j)
    for h in range(1, HALVES):
        for j in order:
            send_panels(h, j)
    fill(fetched, d, d * piece, labels[0])

    panels_t[...] = prolong_ref[...].reshape(rows * BLOCK, W).T
    for h in range(HALVES):
        part[h, tiles] = jnp.zeros((W, wide), jnp.bfloat16)
    load.wait()
    lane = lax.broadcasted_iota(jnp.int32, (1, 2 * BLOCK), 1)

    def place_blocks(i, unused):
        for k in range(0, slots, 2):
            width = min(2, slots - k) * BLOCK
            ids = [
                jnp.where(cols_ref[i, 0, m] >= 0, slot_ref[i, 0, m], -1)
                for m in range(k, min(k + 2, slots))
            ]
            ids = jnp.where(lane < BLOCK, ids[0], ids[-1])[:, :width]
            at = slice(k * BLOCK, k * BLOCK + width)
            values = mat[i, :, at]
            for t in range(tiles):
                mask = jnp.where(ids == t, 1.0, 0.0).astype(jnp.bfloat16)
                spread[i, t * BLOCK : (t + 1) * BLOCK, at] = values * mask
        return unused

    lax.fori_loop(0, rows, place_blocks, 0)

    second = []
    for h in range(HALVES):
        for copy in first[h]:
            copy.wait()

        def one_row(i, unused):
            for k in range(slots):
                col = jnp.maximum(cols_ref[i, 0, k], 0)
                panel = fetched[h][pl.ds(col * sub + lax.div(col, ncap), sub)]
                near[k * BLOCK : (k + 1) * BLOCK, :] = panel.reshape(BLOCK, wide)
            total = jnp.dot(spread[i], near[...], preferred_element_type=jnp.float32)
            top = total.astype(jnp.bfloat16)
            rest = (total - top.astype(jnp.float32)).astype(jnp.bfloat16)
            at = pl.ds(pl.multiple_of(i * BLOCK, BLOCK), BLOCK)
            for t in range(tiles):
                mine_at = slice(t * wide, (t + 1) * wide)
                high[at, mine_at] = top[t * BLOCK : (t + 1) * BLOCK]
                low[at, mine_at] = rest[t * BLOCK : (t + 1) * BLOCK]
            return unused

        lax.fori_loop(0, rows, one_row, 0)

        for v in range(CUTS):
            down = slice(v * tall, (v + 1) * tall)
            left = panels_t[down, :]
            value = jnp.dot(left, high[...], preferred_element_type=jnp.float32)
            value += jnp.dot(left, low[...], preferred_element_type=jnp.float32)
            for t in range(tiles):
                part[h, t, down, :] = value[:, t * wide : (t + 1) * wide].astype(jnp.bfloat16)
            copies = []
            for j in order:
                stage2[h, v, j] = part[h, found[j], down, :]
                copy = pltpu.make_async_remote_copy(
                    src_ref=stage2.at[h, v, j],
                    dst_ref=got2.at[h, v, j],
                    send_sem=send2.at[h, v, j],
                    recv_sem=recv2.at[h, v, j],
                    device_id=(g, lax.rem(d + j, n_dev)),
                    device_id_type=MESH,
                )
                copy.start()
                copies.append(copy)
            got2[h, v, 0] = part[h, found[0], down, :]
            second.append(copies)

    marks = []
    for j in range(n_dev):
        source = lax.rem(d + n_dev - j, n_dev)
        tag = fetched[0][source * piece + ncap * sub]
        marks.append(jnp.max(tag.astype(jnp.float32)))

    third = []
    step = 32
    for n in range(HALVES * CUTS):
        h, v = n // CUTS, n % CUTS
        for copy in second[n]:
            copy.wait()
        copies = []
        for jj in list(range(1, n_grp)) + [0]:
            target = lax.rem(g + jj, n_grp)
            weights = [
                [
                    jnp.where(marks[j] == (target * CT + q).astype(jnp.float32), 1.0, 0.0)
                    for j in range(n_dev)
                ]
                for q in range(CT)
            ]

            def add_up(r, unused):
                at = pl.ds(pl.multiple_of(r * step, step), step)
                sums = [jnp.zeros((step, wide), jnp.float32) for q in range(CT)]
                for j in range(n_dev):
                    value = got2[h, v, j, at, :].astype(jnp.float32)
                    for q in range(CT):
                        sums[q] = sums[q] + value * weights[q][j]
                for q in range(CT):
                    if jj == 0:
                        mine[h, v, q, at, :] = sums[q]
                    else:
                        stage3[h, v, jj, q, at, :] = sums[q].astype(jnp.bfloat16)
                return unused

            lax.fori_loop(0, tall // step, add_up, 0)
            if jj:
                copy = pltpu.make_async_remote_copy(
                    src_ref=stage3.at[h, v, jj],
                    dst_ref=got3.at[h, v, jj],
                    send_sem=send3.at[h, v, jj],
                    recv_sem=recv3.at[h, v, jj],
                    device_id=(target, d),
                    device_id_type=MESH,
                )
                copy.start()
                copies.append(copy)
        third.append(copies)

    saves = []
    for n in range(HALVES * CUTS):
        h, v = n // CUTS, n % CUTS
        for copy in third[n]:
            copy.wait()
        for q in range(CT):
            value = mine[h, v, q]
            for jj in range(1, n_grp):
                value = value + got3[h, v, jj, q].astype(jnp.float32)
            out_ref[n, q] = value
        save = pltpu.make_async_copy(
            out_ref.at[n],
            out_hbm.at[:, pl.ds(v * tall, tall), pl.ds(h * wide, wide)],
            out_sem.at[n],
        )
        save.start()
        saves.append(save)
    for save in saves:
        save.wait()


def far_first(n):
    return sorted(range(1, n), key=lambda j: -min(j, n - j))


def body(blocks, prolong, block_cols, fetch_rows, tile_slot, tile_owner, tile_place):
    n_grp, n_dev = lax.axis_size("grp"), lax.axis_size("dev")
    rows = blocks.shape[2]
    slots = block_cols.shape[3]
    tiles = tile_owner.shape[2]
    ncap = fetch_rows.shape[3]
    if rows * tiles * BLOCK * slots * BLOCK * 2 > 16 * 2**20 or tiles > n_dev:
        return plain_body(
            blocks, prolong, block_cols, fetch_rows, tile_slot, tile_owner, tile_place
        )
    piece = ncap * (BLOCK // LABEL_ROWS) + 1
    wide, tall = W // HALVES, W // CUTS
    bf16, f32 = jnp.bfloat16, jnp.float32
    dma = pltpu.SemaphoreType.DMA
    result = pl.pallas_call(
        functools.partial(kernel, n_grp, n_dev),
        out_shape=jax.ShapeDtypeStruct((CT, W, W), f32),
        in_specs=[pl.BlockSpec(memory_space=pl.ANY)] * 7,
        out_specs=pl.BlockSpec(memory_space=pl.ANY),
        scratch_shapes=[
            pltpu.SMEM((rows, 1, slots), jnp.int32),
            pltpu.SMEM((ncap, 1, n_dev), jnp.int32),
            pltpu.SMEM((rows, 1, slots), jnp.int32),
            pltpu.SMEM((tiles,), jnp.int32),
            pltpu.SMEM((tiles,), jnp.int32),
            pltpu.VMEM((HALVES * CUTS, CT, tall, wide), f32),
            pltpu.VMEM((rows, BLOCK, W), bf16),
            pltpu.VMEM((rows, BLOCK, slots * BLOCK), bf16),
            pltpu.VMEM((n_dev * piece, LABEL_ROWS, wide), bf16),
            pltpu.VMEM((n_dev * piece, LABEL_ROWS, wide), bf16),
            pltpu.VMEM((n_dev, HALVES, piece, LABEL_ROWS, wide), bf16),
            pltpu.VMEM((rows, tiles * BLOCK, slots * BLOCK), bf16),
            pltpu.VMEM((slots * BLOCK, wide), bf16),
            pltpu.VMEM((rows * BLOCK, tiles * wide), bf16),
            pltpu.VMEM((rows * BLOCK, tiles * wide), bf16),
            pltpu.VMEM((W, rows * BLOCK), bf16),
            pltpu.VMEM((HALVES, tiles + 1, W, wide), bf16),
            pltpu.VMEM((HALVES, CUTS, n_dev, tall, wide), bf16),
            pltpu.VMEM((HALVES, CUTS, n_dev, tall, wide), bf16),
            pltpu.VMEM((HALVES, CUTS, n_grp, CT, tall, wide), bf16),
            pltpu.VMEM((HALVES, CUTS, n_grp, CT, tall, wide), bf16),
            pltpu.VMEM((HALVES, CUTS, CT, tall, wide), f32),
            dma,
            dma,
            dma((5,)),
            dma((HALVES * CUTS,)),
            dma((HALVES, n_dev)),
            dma((HALVES, n_dev)),
            dma((HALVES, CUTS, n_dev)),
            dma((HALVES, CUTS, n_dev)),
            dma((HALVES, CUTS, n_grp)),
            dma((HALVES, CUTS, n_grp)),
        ],
        compiler_params=pltpu.CompilerParams(
            collective_id=0, has_side_effects=True, vmem_limit_bytes=62 * 2**20
        ),
    )(
        block_cols[0].transpose(1, 0, 2), fetch_rows[0].transpose(2, 0, 1), tile_slot[0].transpose(1, 0, 2),
        tile_owner[0, 0], tile_place[0, 0], prolong[0, 0], blocks[0, 0],
    )
    return result.reshape(1, 1, CT, W, W)


def solution(mesh):
    return jax.shard_map(
        body,
        mesh=mesh,
        in_specs=(
            P("grp", "dev", None, None, None),
            P("grp", "dev", None, None, None),
            P("grp", "dev", None, None),
            P("grp", "dev", None, None),
            P("grp", "dev", None, None),
            P("grp", "dev", None),
            P("grp", "dev", None),
        ),
        out_specs=P("grp", "dev", None, None, None),
        check_vma=False,
    )
```
